256 devices in a mesh: seg: 128 (over z, y, x), seq: 2 (over core).
Axes of the slice: x: 4, y: 4, z: 8, core: 2. Of those that a mesh axis runs over, the one named last changes fastest.
Arguments:
- latents: float32 [128, 256, 64], P('seg', 'seq'), may hold values from -6 to 6
- steps: int32 [128, 3], P('seg'), may hold values from 1 to 999, as said below
- text_hidden: bfloat16 [384, 2432], replicated, may hold values from -6 to 6
- text_len: int32 [1], replicated, may hold values from 192 to 384
- embed_in: bfloat16 [64, 2432], replicated, may hold values from -0.75 to 0.75
- time_proj: bfloat16 [256, 2432], replicated, may hold values from -0.375 to 0.375
- qkv_image: bfloat16 [2432, 3, 1536], P(None, None, 'seq'), may hold values from -0.125 to 0.125
- kv_text: bfloat16 [2432, 2, 1536], P(None, None, 'seq'), may hold values from -0.125 to 0.125
- out_proj: bfloat16 [1536, 2432], P('seq'), may hold values from -0.15625 to 0.15625
- embed_out: bfloat16 [2432, 64], replicated, may hold values from -0.125 to 0.125
Outputs:
- new_latents: float32 [128, 256, 64], P('seg', 'seq')
The draws below stay inside these ranges and needn't reach their ends.
Inputs may be any that keep to these rules, and one draw needn't show every extreme that they name: `steps`: each row holds a start, a midpoint and an end timestep, strictly falling; a row's end is the next row's start; the first start is 999 and the last end is 1. Text slots from text_len on are padding.
All inputs are finite; a program needn't handle non-finite values.
Results may differ from the reference program's by a relative error of at most 0.0015.
Values may be sent and summed in bfloat16 or wider, within the bound.
No kernel may reach another device: no remote copies, remote signals or barrier semaphores. Data moves between devices by JAX's collectives and lax.ppermute only.
A program may use at most 128 MiB of HBM per device.

```python
import math
import jax
import jax.numpy as jnp
from jax import lax

D = 2432
HEADS = 24
HD = 64
CH = 64
FREQ = 256
TXT = 384
SEGS = 128
IMG = 256


def draw_steps(key, part):
    key = jax.random.fold_in(key, 11)
    inner = jax.random.permutation(key, 997)[:2 * SEGS - 1].astype(jnp.int32) + 2
    falling = -jnp.sort(-inner)
    boundary = jnp.concatenate([jnp.array([999], jnp.int32), falling, jnp.array([1], jnp.int32)])
    segment = jnp.arange(SEGS)
    table = jnp.stack([boundary[2 * segment], boundary[2 * segment + 1], boundary[2 * segment + 2]], axis=1)
    return table.astype(jnp.int32)


def level_of(key, extent, shards, low, top_value):
    gain, own = 1.0, jax.random.fold_in(key, 6)
    for position, parts in shards:
        steps = jnp.exp(jax.random.uniform(jax.random.fold_in(own, position), (parts,), jnp.float32, low / len(shards), top_value / len(shards)))
        gain = gain * jnp.repeat(steps, extent[position] // parts).reshape([-1 if axis == position else 1 for axis in range(len(extent))])
    return gain


def gaussian(rng, shape, spread, most, cuts=(), held_as=jnp.bfloat16):
    values = spread * jax.random.normal(rng, shape, jnp.float32)
    if cuts:
        values = values * level_of(rng, shape, cuts, -0.22, 0.18)
    return jnp.clip(values, -most, most).astype(held_as)


def setup_inputs(seed: int = 0) -> dict:
    keys = jax.random.split(jax.random.key(seed), 11)
    latents = gaussian(keys[0], (SEGS, IMG, CH), 1.0, 6.0, ((0, 128), (1, 2)), jnp.float32)
    steps = draw_steps(jax.random.fold_in(keys[10], 71), 0)
    text_hidden = gaussian(keys[2], (TXT, D), 1.0, 6.0)
    text_len = jax.random.randint(keys[3], (1,), TXT // 2, TXT + 1).astype(jnp.int32)
    embed_in = gaussian(keys[4], (CH, D), CH ** -0.5, 0.75)
    time_proj = gaussian(keys[5], (FREQ, D), FREQ ** -0.5, 0.375)
    qkv_image = gaussian(keys[6], (D, 3, HEADS * HD), D ** -0.5, 0.125, ((2, 2),))
    kv_text = gaussian(keys[7], (D, 2, HEADS * HD), D ** -0.5, 0.125, ((2, 2),))
    out_proj = gaussian(keys[8], (HEADS * HD, D), (HEADS * HD) ** -0.5, 0.15625, ((0, 2),))
    embed_out = gaussian(keys[9], (D, CH), D ** -0.5, 0.125)
    return dict(latents=latents, steps=steps, text_hidden=text_hidden, text_len=text_len, embed_in=embed_in, time_proj=time_proj, qkv_image=qkv_image, kv_text=kv_text, out_proj=out_proj, embed_out=embed_out)


epsilon = 1e-06

def layer_norm(hidden):
    average = lax.optimization_barrier(jnp.mean(hidden, -1, keepdims=True))
    centred = hidden - average
    return centred * lax.rsqrt(lax.optimization_barrier(jnp.mean(centred * centred, -1, keepdims=True)) + epsilon)

def rms_heads(values, head_size):
    rows = values.shape[0]
    shaped = values.reshape(rows, -1, head_size)
    shaped = shaped * lax.rsqrt(lax.optimization_barrier(jnp.mean(shaped * shaped, -1, keepdims=True)) + epsilon)
    return shaped.reshape(rows, -1)

def time_embed(time_value, width):
    half_width = width // 2
    frequency = jnp.exp(-math.log(10000.0) * jnp.arange(half_width, dtype=jnp.float32) / half_width)
    angles = time_value * frequency
    return jnp.concatenate([jnp.cos(angles), jnp.sin(angles)])

def velocity(latent, time_value, text_hidden, text_len, embed_in, time_proj, qkv_image, kv_text, out_proj, embed_out):
    emb_vec = time_embed(time_value, time_proj.shape[0]).astype(jnp.bfloat16)
    time_vec = jnp.dot(emb_vec[None, :], time_proj, preferred_element_type=jnp.float32)
    hidden = jnp.dot(latent.astype(jnp.bfloat16), embed_in, preferred_element_type=jnp.float32) + time_vec
    normed = layer_norm(hidden).astype(jnp.bfloat16)
    full_width = qkv_image.shape[2]
    projected = jnp.dot(normed, qkv_image.reshape(D, 3 * full_width), preferred_element_type=jnp.float32)
    queries = rms_heads(projected[:, :full_width], HD).astype(jnp.bfloat16)
    key_img = rms_heads(projected[:, full_width:2 * full_width], HD).astype(jnp.bfloat16)
    val_img = projected[:, 2 * full_width:].astype(jnp.bfloat16)
    text_norm = layer_norm(text_hidden.astype(jnp.float32) + time_vec).astype(jnp.bfloat16)
    text_proj = jnp.dot(text_norm, kv_text.reshape(D, 2 * full_width), preferred_element_type=jnp.float32)
    key_txt = rms_heads(text_proj[:, :full_width], HD).astype(jnp.bfloat16)
    val_txt = text_proj[:, full_width:].astype(jnp.bfloat16)
    all_keys = jnp.concatenate([key_img, key_txt], 0)
    all_values = jnp.concatenate([val_img, val_txt], 0)
    live_text = (jnp.arange(TXT) < text_len[0]).astype(jnp.float32)
    live_mask = jnp.concatenate([jnp.ones((IMG,), jnp.float32), live_text])
    rows = queries.shape[0]
    q_heads = queries.astype(jnp.float32).reshape(rows, HEADS, HD)
    k_heads = all_keys.astype(jnp.float32).reshape(-1, HEADS, HD)
    v_heads = all_values.astype(jnp.float32).reshape(-1, HEADS, HD)
    scores = jnp.einsum('qhd,khd->hqk', q_heads, k_heads) / math.sqrt(HD)
    weight = jnp.exp(scores) * live_mask[None, None, :]
    totals = lax.optimization_barrier(jnp.sum(weight, -1, keepdims=True))
    probability = (weight / totals).astype(jnp.bfloat16)
    attended = jnp.einsum('hqk,khd->qhd', probability.astype(jnp.float32), v_heads)
    attended = attended.reshape(rows, full_width).astype(jnp.bfloat16)
    mixed_out = jnp.dot(attended, out_proj, preferred_element_type=jnp.float32)
    residual = hidden + mixed_out
    return jnp.dot(layer_norm(residual).astype(jnp.bfloat16), embed_out, preferred_element_type=jnp.float32)

def reference(latents, steps, text_hidden, text_len, embed_in, time_proj, qkv_image, kv_text, out_proj, embed_out):
    weights_all = (text_hidden, text_len, embed_in, time_proj, qkv_image, kv_text, out_proj, embed_out)

    def segment_work(pair):
        latent, step_row = pair
        times = step_row.astype(jnp.float32)
        sigma_start = times[0] / 1000.0
        sigma_mid = times[1] / 1000.0
        sigma_end = times[2] / 1000.0
        first_vel = velocity(latent, times[0], *weights_all)
        midpoint = latent + (sigma_mid - sigma_start) * first_vel
        second_vel = velocity(midpoint, times[1], *weights_all)
        fine_end = midpoint + (sigma_end - sigma_mid) * second_vel
        return (fine_end, sigma_end / sigma_start)
    fine_all, shrink_all = lax.map(segment_work, (latents, steps))

    def chain_step(earlier, segment_in):
        fine_end, shrink, latent = segment_in
        updated = shrink * earlier + (fine_end - shrink * latent)
        return (updated, updated)
    first_end = fine_all[0]
    _, later_ends = lax.scan(chain_step, first_end, (fine_all[1:], shrink_all[1:], latents[1:]))
    return jnp.concatenate([first_end[None], later_ends], 0)
```

```python
import math

import jax
import jax.numpy as jnp
from jax import lax
from jax.sharding import PartitionSpec as P

HD = 64


epsilon = 1e-06


def scan_rounds(count, shape):
    rounds = []
    base = 1
    for extent in shape:
        width = 1
        while width < extent:
            step = base * width
            pairs = []
            for me in range(count):
                place = (me // base) % extent
                block = place // (2 * width) * (2 * width)
                partner = block + 2 * width - 1 - (place - block)
                pairs.append((me, me + (partner - place) * base))
            rounds.append((pairs, step))
            width *= 2
        base *= extent
    return rounds


def prefix_sum(value, axis):
    count, mine = lax.axis_size(axis), lax.axis_index(axis)
    shape, left = [], count
    while left > 1:
        extent = 4 if left % 4 == 0 and len(shape) < 2 else left
        shape.append(extent)
        left //= extent
    total = running = value
    for pairs, step in scan_rounds(count, shape):
        came = lax.ppermute(total, axis, pairs)
        later = (mine // step) % 2 == 1
        running = running + jnp.where(later, came, 0.0)
        total = total + came
    return running


def layer_norm(hidden):
    average = jnp.mean(hidden, -1, keepdims=True)
    centred = hidden - average
    return centred * lax.rsqrt(jnp.mean(centred * centred, -1, keepdims=True) + epsilon)


def rms_heads(values, head_size):
    rows = values.shape[0]
    shaped = values.reshape(rows, -1, head_size)
    shaped = shaped * lax.rsqrt(jnp.mean(shaped * shaped, -1, keepdims=True) + epsilon)
    return shaped.reshape(rows, -1)


def time_embed(time_value, width):
    half_width = width // 2
    frequency = jnp.exp(-math.log(10000.0) * jnp.arange(half_width, dtype=jnp.float32) / half_width)
    angles = time_value * frequency
    return jnp.concatenate([jnp.cos(angles), jnp.sin(angles)])


def attend(queries, all_keys, all_values, live_mask, head_total, head_size):
    pieces = []
    for head_index in range(head_total):
        low = head_index * head_size
        high = low + head_size
        scores = jnp.einsum(
            "qd,kd->qk",
            queries[:, low:high],
            all_keys[:, low:high],
            preferred_element_type=jnp.float32,
        ) / math.sqrt(head_size)
        weight = jnp.exp(scores) * live_mask[None, :]
        totals = jnp.sum(weight, -1, keepdims=True)
        probability = (weight / totals).astype(jnp.bfloat16)
        pieces.append(
            jnp.dot(probability, all_values[:, low:high], preferred_element_type=jnp.float32)
        )
    return jnp.concatenate(pieces, 1).astype(jnp.bfloat16)


def per_device(
    latents,
    steps,
    text_hidden,
    text_len,
    embed_in,
    time_proj,
    qkv_image,
    kv_text,
    out_proj,
    embed_out,
):
    local_width = qkv_image.shape[2]
    local_heads = local_width // HD
    model_width = qkv_image.shape[0]
    qkv_flat = qkv_image.reshape(model_width, 3 * local_width)
    kv_flat = kv_text.reshape(model_width, 2 * local_width)
    text_slots = text_hidden.shape[0]
    live_text = (jnp.arange(text_slots) < text_len[0]).astype(jnp.float32)

    def velocity(latent, time_value):
        emb_vec = time_embed(time_value, time_proj.shape[0]).astype(jnp.bfloat16)
        time_vec = jnp.dot(emb_vec[None, :], time_proj, preferred_element_type=jnp.float32)
        hidden = (
            jnp.dot(latent.astype(jnp.bfloat16), embed_in, preferred_element_type=jnp.float32)
            + time_vec
        )
        normed = layer_norm(hidden).astype(jnp.bfloat16)
        projected = jnp.dot(
            lax.all_gather(normed, "seq", axis=0, tiled=True),
            qkv_flat,
            preferred_element_type=jnp.float32,
        )
        queries = rms_heads(projected[:, :local_width], HD).astype(jnp.bfloat16)
        key_img = rms_heads(projected[:, local_width : 2 * local_width], HD).astype(jnp.bfloat16)
        val_img = projected[:, 2 * local_width :].astype(jnp.bfloat16)
        text_norm = layer_norm(text_hidden.astype(jnp.float32) + time_vec).astype(jnp.bfloat16)
        text_proj = jnp.dot(text_norm, kv_flat, preferred_element_type=jnp.float32)
        key_txt = rms_heads(text_proj[:, :local_width], HD).astype(jnp.bfloat16)
        val_txt = text_proj[:, local_width:].astype(jnp.bfloat16)
        all_keys = jnp.concatenate([key_img, key_txt], 0)
        all_values = jnp.concatenate([val_img, val_txt], 0)
        live_mask = jnp.concatenate([jnp.ones((projected.shape[0],), jnp.float32), live_text])
        attended = attend(queries, all_keys, all_values, live_mask, local_heads, HD)
        mixed_out = lax.psum_scatter(
            jnp.dot(attended, out_proj, preferred_element_type=jnp.float32).astype(jnp.bfloat16),
            "seq",
            scatter_dimension=0,
            tiled=True,
        ).astype(jnp.float32)
        residual = hidden + mixed_out
        return jnp.dot(
            layer_norm(residual).astype(jnp.bfloat16), embed_out, preferred_element_type=jnp.float32
        )

    latent = latents[0]
    times = steps[0].astype(jnp.float32)
    sigma_start = times[0] / 1000.0
    sigma_mid = times[1] / 1000.0
    sigma_end = times[2] / 1000.0
    first_vel = velocity(latent, times[0])
    midpoint = latent + (sigma_mid - sigma_start) * first_vel
    second_vel = velocity(midpoint, times[1])
    fine_end = midpoint + (sigma_end - sigma_mid) * second_vel
    shrink = sigma_end / sigma_start
    segment = lax.axis_index("seg")
    offset = jnp.where(segment == 0, fine_end, fine_end - shrink * latent)
    result = sigma_end * prefix_sum(offset.T / sigma_end, "seg").T
    return result[None]


def solution(mesh):
    return jax.shard_map(
        per_device,
        mesh=mesh,
        in_specs=(
            P("seg", "seq", None),
            P("seg", None),
            P(),
            P(),
            P(),
            P(),
            P(None, None, "seq"),
            P(None, None, "seq"),
            P("seq", None),
            P(),
        ),
        out_specs=P("seg", "seq", None),
        check_vma=False,
    )
```

```python
import math

import jax
import jax.numpy as jnp
import numpy as np
from jax import lax
from jax.experimental import pallas as pl
from jax.experimental.pallas import tpu as pltpu
from jax.sharding import PartitionSpec as P

HD = 64
CHUNK = 256
AUX = 16
epsilon = 1e-06
F32 = jnp.float32
BF16 = jnp.bfloat16


def dot(a, b):
    return jnp.dot(a, b, preferred_element_type=F32)


def dot_t(a, b):
    return lax.dot_general(a, b, (((1,), (1,)), ((), ())), preferred_element_type=F32)


def row_stats(x):
    mean = jnp.mean(x, -1, keepdims=True)
    centred = x - mean
    return mean, lax.rsqrt(jnp.mean(centred * centred, -1, keepdims=True) + epsilon)


def head_means():
    row = lax.broadcasted_iota(jnp.int32, (CHUNK, CHUNK), 0) // HD
    col = lax.broadcasted_iota(jnp.int32, (CHUNK, CHUNK), 1) // HD
    return jnp.where(row == col, 1.0 / HD, 0.0).astype(BF16)


def rms_heads(y, means):
    square = y * y
    high = square.astype(BF16)
    low = (square - high.astype(F32)).astype(BF16)
    return y * lax.rsqrt(dot(high, means) + dot(low, means) + epsilon)


def prepare_kernel(
    steps, text_len, frequency, time_proj, embed_in, text, kv, qkv,
    time_out, key0, key1, val0, val1, mixed_in, mixed_time,
    kv_buf, qkv_buf, text_rows, embed_rows, stats, embed_mean, sems,
):
    parts = kv.shape[2] // CHUNK
    kv_chunks, qkv_chunks = 2 * parts, 3 * parts

    def kv_copy(i):
        return pltpu.make_async_copy(
            kv.at[i // parts, :, pl.ds(i % parts * CHUNK, CHUNK)], kv_buf.at[i], sems.at[i]
        )

    def qkv_copy(i):
        return pltpu.make_async_copy(
            qkv.at[i // parts, :, pl.ds(i % parts * CHUNK, CHUNK)],
            qkv_buf.at[i],
            sems.at[kv_chunks + i],
        )

    for i in range(kv_chunks):
        kv_copy(i).start()
    for i in range(qkv_chunks):
        qkv_copy(i).start()

    row = lax.broadcasted_iota(jnp.int32, (AUX, 1), 0)
    t0, t1 = steps[0, 0].astype(F32), steps[0, 1].astype(F32)
    angle = jnp.where(row % 2 == 0, t0, t1) * frequency[...]
    emb = jnp.concatenate([jnp.cos(angle), jnp.sin(angle)], 1).astype(BF16)
    time_vec = dot(emb, time_proj[...])
    time_out[...] = time_vec[:8]
    high = time_vec.astype(BF16).astype(F32)
    aux = jnp.where(
        row < 2, high, jnp.where(row < 4, time_vec - high, jnp.where(row == 4, 1.0, 0.0))
    ).astype(BF16)
    slots = text.shape[0]
    text_rows[:slots] = text[...]
    text_rows[slots:] = aux
    channels = embed_in.shape[0]
    embed_rows[:channels] = embed_in[...]
    embed_rows[channels:] = aux
    time_mean = jnp.mean(time_vec, -1, keepdims=True)
    embed_mean[...] = jnp.broadcast_to(
        jnp.mean(embed_in[...].astype(F32), -1, keepdims=True), embed_mean.shape
    )
    words = text[...].astype(F32)
    for t in range(2):
        mean, scale = row_stats(words + time_vec[t : t + 1])
        stats[2 * t] = jnp.broadcast_to(mean, stats.shape[1:])
        stats[2 * t + 1] = jnp.broadcast_to(scale, stats.shape[1:])
    means = head_means()
    live = lax.broadcasted_iota(jnp.int32, (slots, CHUNK), 0) < text_len[0]

    def text_part(i):
        kv_copy(i).wait()
        out = dot(text_rows[...], kv_buf[i])
        ones = out[slots + 4 : slots + 5]
        result = []
        for t in range(2):
            of_time = out[slots + t : slots + t + 1] + out[slots + 2 + t : slots + 3 + t]
            mean = jnp.tile(stats[2 * t], (1, CHUNK // 128))
            scale = jnp.tile(stats[2 * t + 1], (1, CHUNK // 128))
            result.append(scale * (out[:slots] + of_time - mean * ones))
        return result

    def key_chunk(i, _):
        at = pl.ds(pl.multiple_of(i * CHUNK, CHUNK), CHUNK)
        for y, ref in zip(text_part(i), (key0, key1)):
            ref[:, at] = rms_heads(y, means).astype(BF16)
        return 0

    def val_chunk(i, _):
        at = pl.ds(pl.multiple_of(i * CHUNK, CHUNK), CHUNK)
        for y, ref in zip(text_part(parts + i), (val0, val1)):
            ref[:, at] = jnp.where(live, y, 0.0).astype(BF16)
        return 0

    def image_chunk(i, _):
        qkv_copy(i).wait()
        at = pl.ds(pl.multiple_of(i * CHUNK, CHUNK), CHUNK)
        out = dot(embed_rows[...], qkv_buf[i])
        ones = out[channels + 4 : channels + 5]
        of_embed = out[:channels] - jnp.tile(embed_mean[...], (1, CHUNK // 128)) * ones
        top = of_embed.astype(BF16)
        mixed_in[:channels, at] = top
        mixed_in[channels:, at] = (of_embed - top.astype(F32)).astype(BF16)
        of_time = out[channels : channels + 8]
        later = out[channels + 2 : channels + 4]
        both = of_time[:2] + later - time_mean[:2] * ones
        mixed_time[:, at] = jnp.concatenate([both, jnp.zeros((6, CHUNK), F32)], 0)
        return 0

    lax.fori_loop(0, parts, key_chunk, 0)
    lax.fori_loop(0, parts, val_chunk, 0)
    lax.fori_loop(0, qkv_chunks, image_chunk, 0)


def attend_kernel(
    t, text_len, mine, other, embed_in, time_vec, mixed_in, mixed_time, text_key, text_val,
    out_mine, out_other, qkv,
):
    width = text_key.shape[1]
    tokens = mine.shape[1]
    slots = text_key.shape[0]
    latent = jnp.concatenate([mine[...], other[...]], 1).T.astype(BF16)
    hidden = dot(latent, embed_in[...]) + time_vec[t : t + 1]
    _, scale = row_stats(hidden)
    twice = jnp.concatenate([latent, latent], 1)
    means = head_means()
    for i in range(3 * width // CHUNK):
        at = slice(i * CHUNK, (i + 1) * CHUNK)
        y = scale * (dot(twice, mixed_in[:, at]) + mixed_time[t : t + 1, at])
        if i < 2 * width // CHUNK:
            y = rms_heads(y, means)
        if i < width // CHUNK:
            y = y * (1.0 / math.sqrt(HD))
        qkv[:, at] = y.astype(BF16)
    lane = lax.broadcasted_iota(jnp.int32, (2 * tokens, 2 * HD), 1)
    first = lane < HD
    live = (
        lax.broadcasted_iota(jnp.int32, (slots, 2 * HD), 0) < text_len[0]
    ).astype(BF16)
    always = jnp.ones((2 * tokens, 2 * HD), BF16)
    for pair in range(width // (2 * HD)):
        at = slice(pair * 2 * HD, (pair + 1) * 2 * HD)
        q = qkv[:, at]
        both = jnp.concatenate([jnp.where(first, q, 0), jnp.where(first, 0, q)], 0)
        image_key = qkv[:, width + pair * 2 * HD : width + (pair + 1) * 2 * HD]
        image_val = qkv[:, 2 * width + pair * 2 * HD : 2 * width + (pair + 1) * 2 * HD]
        p_image = jnp.exp(dot_t(both, image_key)).astype(BF16)
        p_text = jnp.exp(dot_t(both, text_key[:, at])).astype(BF16)
        out = dot(p_image, jnp.concatenate([image_val, always], 1)) + dot(
            p_text, jnp.concatenate([text_val[:, at], live], 1)
        )
        out = out[:, : 2 * HD] / out[:, 2 * HD :]
        out = jnp.where(first, out[: 2 * tokens], out[2 * tokens :]).astype(BF16)
        out_mine[:, at] = out[:tokens]
        out_other[:, at] = out[tokens:]


def output_kernel(
    t, steps, mine, came, latent, embed_in, time_vec, proj_mine, proj_other, embed_out,
    *rest,
):
    if t == 0:
        result, proj, sems = rest
    else:
        start, result, proj, sems = rest
    rows = proj_mine.shape[0]
    parts = rows // CHUNK
    copies = []
    for i in range(2 * parts):
        src = proj_mine if i < parts else proj_other
        copies.append(
            pltpu.make_async_copy(
                src.at[pl.ds(i % parts * CHUNK, CHUNK)], proj.at[pl.ds(i * CHUNK, CHUNK)], sems.at[i]
            )
        )
        copies[-1].start()
    residual = dot(latent[...].T.astype(BF16), embed_in[...]) + time_vec[t : t + 1]
    for i in range(2 * parts):
        src = mine if i < parts else came
        copies[i].wait()
        residual = residual + dot(
            src[:, i % parts * CHUNK : (i % parts + 1) * CHUNK],
            proj[i * CHUNK : (i + 1) * CHUNK],
        )
    mean, scale = row_stats(residual)
    normed = ((residual - mean) * scale).astype(BF16)
    velocity = dot_t(embed_out[...], normed)
    a, m, b = (steps[0, k].astype(F32) / 1000.0 for k in range(3))
    if t == 0:
        result[...] = latent[...] + (m - a) * velocity
    else:
        fine = latent[...] + (b - m) * velocity
        segment = lax.axis_index("seg")
        offset = jnp.where(segment == 0, fine, fine - b / a * start[...])
        result[...] = offset / b


def scan_rounds(count, shape):
    rounds = []
    base = 1
    for extent in shape:
        width = 1
        while width < extent:
            step = base * width
            pairs = []
            for me in range(count):
                place = (me // base) % extent
                block = place // (2 * width) * (2 * width)
                partner = block + 2 * width - 1 - (place - block)
                pairs.append((me, me + (partner - place) * base))
            rounds.append((pairs, step))
            width *= 2
        base *= extent
    return rounds


def prefix_sum(value, axis):
    count, mine = lax.axis_size(axis), lax.axis_index(axis)
    shape, left = [], count
    while left > 1:
        extent = 4 if left % 4 == 0 and len(shape) < 2 else left
        shape.append(extent)
        left //= extent
    total = running = value
    for pairs, step in scan_rounds(count, shape):
        came = lax.ppermute(total, axis, pairs)
        later = (mine // step) % 2 == 1
        running = running + jnp.where(later, came, 0.0)
        total = total + came
    return running


VMEM = pl.BlockSpec(memory_space=pltpu.VMEM)
SMEM = pl.BlockSpec(memory_space=pltpu.SMEM)
ANY = pl.BlockSpec(memory_space=pl.ANY)


def per_device(
    latents, steps, text_hidden, text_len, embed_in, time_proj, qkv_image, kv_text, out_proj, embed_out
):
    model, _, width = qkv_image.shape
    slots = text_hidden.shape[0]
    channels = embed_in.shape[0]
    tokens = latents.shape[1]
    swap = [(0, 1), (1, 0)]
    half = time_proj.shape[0] // 2
    frequency = np.exp(-math.log(10000.0) * np.arange(half) / half).astype(np.float32)[None]
    latent = latents[0].T
    other = lax.ppermute(latent, "seq", swap)
    proj_other = lax.ppermute(out_proj, "seq", swap)
    embed_out_t = embed_out.T
    qkv = jnp.transpose(qkv_image, (1, 0, 2))
    kv = jnp.transpose(kv_text, (1, 0, 2))
    chunks = width // CHUNK

    def shape(dims, dtype):
        return jax.ShapeDtypeStruct(dims, dtype)

    time_vec, key0, key1, val0, val1, mixed_in, mixed_time = pl.pallas_call(
        prepare_kernel,
        out_shape=(
            shape((8, model), F32),
            *[shape((slots, width), BF16)] * 4,
            shape((2 * channels, 3 * width), BF16),
            shape((8, 3 * width), F32),
        ),
        in_specs=[SMEM, SMEM, VMEM, VMEM, VMEM, VMEM, ANY, ANY],
        out_specs=[VMEM] * 7,
        scratch_shapes=[
            pltpu.VMEM((2 * chunks, model, CHUNK), BF16),
            pltpu.VMEM((3 * chunks, model, CHUNK), BF16),
            pltpu.VMEM((slots + AUX, model), BF16),
            pltpu.VMEM((channels + AUX, model), BF16),
            pltpu.VMEM((4, slots, 128), F32),
            pltpu.VMEM((channels, 128), F32),
            pltpu.SemaphoreType.DMA((5 * chunks,)),
        ],
        compiler_params=pltpu.CompilerParams(vmem_limit_bytes=48 << 20),
        name="prepare",
    )(steps, text_len, frequency, time_proj, embed_in, text_hidden, kv, qkv)

    def attend(t, mine, other, text_key, text_val):
        return pl.pallas_call(
            lambda *refs: attend_kernel(t, *refs),
            out_shape=(shape((tokens, width), BF16),) * 2,
            in_specs=[SMEM] + [VMEM] * 8,
            out_specs=[VMEM] * 2,
            scratch_shapes=[pltpu.VMEM((2 * tokens, 3 * width), BF16)],
            compiler_params=pltpu.CompilerParams(vmem_limit_bytes=32 << 20),
            name="attend",
        )(text_len, mine, other, embed_in, time_vec, mixed_in, mixed_time, text_key, text_val)

    def output(t, mine, came, now, *start):
        return pl.pallas_call(
            lambda *refs: output_kernel(t, *refs),
            out_shape=shape((channels, tokens), F32),
            in_specs=[SMEM] + [VMEM] * 5 + [ANY] * 2 + [VMEM] * (1 + len(start)),
            out_specs=VMEM,
            scratch_shapes=[
                pltpu.VMEM((2 * width, model), BF16),
                pltpu.SemaphoreType.DMA((2 * chunks,)),
            ],
            compiler_params=pltpu.CompilerParams(vmem_limit_bytes=32 << 20),
            name="output",
        )(steps, mine, came, now, embed_in, time_vec, out_proj, proj_other, embed_out_t, *start)

    mine, theirs = attend(0, latent, other, key0, val0)
    middle = output(0, mine, lax.ppermute(theirs, "seq", swap), latent)
    mine, theirs = attend(1, middle, lax.ppermute(middle, "seq", swap), key1, val1)
    offset = output(1, mine, lax.ppermute(theirs, "seq", swap), middle, latent)
    result = steps[0, 2].astype(F32) / 1000.0 * prefix_sum(offset, "seg")
    return result.T[None]


def solution(mesh):
    return jax.shard_map(
        per_device,
        mesh=mesh,
        in_specs=(
            P("seg", "seq", None),
            P("seg", None),
            P(),
            P(),
            P(),
            P(),
            P(None, None, "seq"),
            P(None, None, "seq"),
            P("seq", None),
            P(),
        ),
        out_specs=P("seg", "seq", None),
        check_vma=False,
    )
```

```python
import math

import jax
import jax.numpy as jnp
import numpy as np
from jax import lax
from jax.experimental import pallas as pl
from jax.experimental.pallas import tpu as pltpu
from jax.sharding import PartitionSpec as P

HD = 64
CHUNK = 256
AUX = 16
epsilon = 1e-06
F32 = jnp.float32
BF16 = jnp.bfloat16


def dot(a, b):
    return jnp.dot(a, b, preferred_element_type=F32)


def dot_t(a, b):
    return lax.dot_general(a, b, (((1,), (1,)), ((), ())), preferred_element_type=F32)


def row_stats(x):
    mean = jnp.mean(x, -1, keepdims=True)
    centred = x - mean
    return mean, lax.rsqrt(jnp.mean(centred * centred, -1, keepdims=True) + epsilon)


def head_means():
    row = lax.broadcasted_iota(jnp.int32, (CHUNK, CHUNK), 0) // HD
    col = lax.broadcasted_iota(jnp.int32, (CHUNK, CHUNK), 1) // HD
    return jnp.where(row == col, 1.0 / HD, 0.0).astype(BF16)


def head_scale(y, means, scale):
    square = y * y
    high = square.astype(BF16)
    low = (square - high.astype(F32)).astype(BF16)
    mean = dot(high, means) + dot(low, means)
    return scale * lax.rsqrt(mean * (scale * scale) + epsilon)


def split(x):
    high = x.astype(BF16)
    return high, (x - high.astype(F32)).astype(BF16)


def time_rows(x, fifth=0.0):
    high, low = (part.astype(F32) for part in split(x))
    row = lax.broadcasted_iota(jnp.int32, (AUX, 1), 0)
    parts = (high[:1], low[:1], high[1:], low[1:], fifth)
    out = jnp.zeros((AUX, x.shape[1]), F32)
    for k, part in enumerate(parts):
        out = jnp.where(row == k, part, out)
    return out.astype(BF16)


def latent_rows(t, latent):
    z = latent.T.astype(BF16)
    col = lax.broadcasted_iota(jnp.int32, (z.shape[0], AUX), 1)
    pick = jnp.where(col // 2 == t, 1.0, 0.0).astype(BF16)
    return jnp.concatenate([z, z, pick], 1)


def prepare_kernel(
    steps, text_len, frequency, time_proj, embed_in, text, qkv, kv,
    mixed_embed, mixed_in, key0, key1, val0, val1,
    time_buf, embed_buf, text_rows, qkv_buf, kv_raw, kv_buf, embed_rows, stats, sems,
):
    parts = qkv.shape[2] // CHUNK
    slots, model = text.shape
    channels = embed_in.shape[0]
    copies = [
        pltpu.make_async_copy(time_proj, time_buf, sems.at[0]),
        pltpu.make_async_copy(embed_in, embed_buf, sems.at[1]),
        pltpu.make_async_copy(text, text_rows.at[pl.ds(0, slots)], sems.at[2]),
    ]
    steps_in = 3 * parts
    share = -(-model // steps_in // 16) * 16
    kv_rows = [(i * share, min(share, model - i * share)) for i in range(steps_in)]
    for i in range(steps_in):
        copies.append(
            pltpu.make_async_copy(
                qkv.at[i // parts, :, pl.ds(i % parts * CHUNK, CHUNK)], qkv_buf.at[i], sems.at[3 + i]
            )
        )
    kv_copies = []
    for i, (low, size) in enumerate(kv_rows):
        at = pl.ds(low, size)
        kv_copies.append(
            pltpu.make_async_copy(kv.at[at], kv_raw.at[at], sems.at[3 + steps_in + i])
        )
    for copy in copies[:2]:
        copy.start()
    for i in range(steps_in):
        kv_copies[i].start()
        copies[3 + i].start()
    copies[2].start()
    means = head_means()
    row = lax.broadcasted_iota(jnp.int32, (AUX, 1), 0)
    t0, t1 = steps[0, 0].astype(F32), steps[0, 1].astype(F32)
    angle = jnp.where(row % 2 == 0, t0, t1) * frequency[...]
    emb = jnp.concatenate([jnp.cos(angle), jnp.sin(angle)], 1).astype(BF16)
    copies[0].wait()
    time_vec = dot(emb, time_buf[...])
    high = time_vec.astype(BF16).astype(F32)
    aux = jnp.where(
        row < 2, high, jnp.where(row < 4, time_vec - high, jnp.where(row == 4, 1.0, 0.0))
    ).astype(BF16)
    time_mean = jnp.mean(time_vec[:2], -1, keepdims=True)
    time_centred = time_vec[:2] - time_mean
    of_times = jnp.mean(time_centred * time_centred, -1, keepdims=True)
    copies[1].wait()
    embed = embed_buf[...]
    embed_rows[:channels] = embed
    embed_rows[channels:] = aux
    embed_mean = jnp.mean(embed.astype(F32), -1, keepdims=True)

    def store_mixed(ref, at, of_embed, of_time):
        high, low = split(of_embed)
        ref[:channels, at] = high
        ref[channels : 2 * channels, at] = low
        ref[2 * channels :, at] = time_rows(of_time)

    store_mixed(mixed_embed, slice(None), embed.astype(F32) - embed_mean, time_centred)
    for i, (low, size) in enumerate(kv_rows):
        kv_copies[i].wait()
        copies[3 + i].wait()
        kv_buf[:, low : low + size] = jnp.swapaxes(kv_raw[low : low + size], 0, 1)
        at = slice(i * CHUNK, (i + 1) * CHUNK)
        out = dot(embed_rows[...], qkv_buf[i])
        ones = out[channels + 4 : channels + 5]
        of_time = out[channels : channels + 2] + out[channels + 2 : channels + 4]
        store_mixed(mixed_in, at, out[:channels] - embed_mean * ones, of_time - time_mean * ones)

    text_rows[slots:] = aux
    copies[2].wait()

    sums = dot_t(text_rows[:slots], time_rows(time_centred, 1.0))
    word_mean = sums[:, 4:5] * (1.0 / model)
    block = 48
    for i in range(slots // block):
        here = slice(i * block, (i + 1) * block)
        centred = text_rows[here].astype(F32) - word_mean[here]
        own = jnp.mean(centred * centred, -1, keepdims=True)
        for t in range(2):
            cross = (sums[here, 2 * t : 2 * t + 1] + sums[here, 2 * t + 1 : 2 * t + 2]) * (2.0 / model)
            scale = lax.rsqrt(own + cross + of_times[t : t + 1] + epsilon)
            stats[t, here] = jnp.broadcast_to(scale, (block, 128))

    live = lax.broadcasted_iota(jnp.int32, (slots, CHUNK), 0) < text_len[0]

    def text_project(i):
        return dot(text_rows[...], kv_buf[i // parts, :, i % parts * CHUNK : (i % parts + 1) * CHUNK])

    def text_store(i, out):
        at = slice(i % parts * CHUNK, (i % parts + 1) * CHUNK)
        ones = out[slots + 4 : slots + 5]
        base = out[:slots] - word_mean * ones
        for t in range(2):
            of_time = out[slots + t : slots + t + 1] + out[slots + 2 + t : slots + 3 + t]
            y = base + (of_time - time_mean[t : t + 1] * ones)
            scale = stats[t][:, :1]
            if i < parts:
                (key0, key1)[t][:, at] = (y * head_scale(y, means, scale)).astype(BF16)
            else:
                (val0, val1)[t][:, at] = jnp.where(live, y * scale, 0.0).astype(BF16)

    for i in range(2 * parts):
        text_store(i, text_project(i))


def attend(qkv, rows, text_len, text_key, text_val, store):
    width = text_key.shape[1]
    slots = text_key.shape[0]
    tokens = rows.stop - rows.start
    pair_width = 2 * HD
    first = lax.broadcasted_iota(jnp.int32, (tokens, pair_width), 1) < HD
    live = (lax.broadcasted_iota(jnp.int32, (slots, pair_width), 0) < text_len[0]).astype(BF16)
    always = jnp.ones((qkv.shape[0], pair_width), BF16)
    for pair in range(width // pair_width):
        at = slice(pair * pair_width, (pair + 1) * pair_width)
        q = qkv[rows, at]
        both = jnp.concatenate([jnp.where(first, q, 0), jnp.where(first, 0, q)], 0)
        image_key = qkv[:, width + at.start : width + at.stop]
        image_val = qkv[:, 2 * width + at.start : 2 * width + at.stop]
        p_image = jnp.exp2(dot_t(both, image_key)).astype(BF16)
        p_text = jnp.exp2(dot_t(both, text_key[:, at])).astype(BF16)
        out = dot(p_image, jnp.concatenate([image_val, always], 1)) + dot(
            p_text, jnp.concatenate([text_val[:, at], live], 1)
        )
        out = out[:, :pair_width] / out[:, pair_width:]
        store(at, jnp.where(first, out[:tokens], out[tokens:]).astype(BF16))


def theirs_kernel(
    t, text_len, mine, other, mixed_embed, mixed_in, text_key, text_val, qkv, out_other
):
    width = text_key.shape[1]
    tokens = mine.shape[1]
    rows = latent_rows(t, jnp.concatenate([mine[...], other[...]], 1))
    centred = dot(rows, mixed_embed[...])
    scale = lax.rsqrt(jnp.mean(centred * centred, -1, keepdims=True) + epsilon)
    means = head_means()
    for i in range(3 * width // CHUNK):
        at = slice(i * CHUNK, (i + 1) * CHUNK)
        y = dot(rows, mixed_in[:, at])
        if i < 2 * width // CHUNK:
            of_head = head_scale(y, means, scale)
            if i < width // CHUNK:
                of_head = of_head * (math.log2(math.e) / math.sqrt(HD))
            y = y * of_head
        else:
            y = y * scale
        qkv[:, at] = y.astype(BF16)

    def store(at, value):
        out_other[:, at] = value

    attend(qkv, slice(tokens, 2 * tokens), text_len, text_key, text_val, store)


def mine_kernel(
    t, text_len, qkv, mine, mixed_embed, text_key, text_val, proj_mine, residual, attended
):
    tokens = mine.shape[1]

    def store(at, value):
        attended[:, at] = value

    attend(qkv, slice(0, tokens), text_len, text_key, text_val, store)
    rows = latent_rows(t, mine[...])
    residual[...] = dot(rows, mixed_embed[...]) + dot(attended[...], proj_mine[...])


def output_kernel(t, steps, residual, came, latent, proj_other, embed_out, *rest):
    result = rest[-1]
    whole = residual[...] + dot(came[...], proj_other[...])
    mean, scale = row_stats(whole)
    normed = ((whole - mean) * scale).astype(BF16)
    velocity = dot_t(embed_out[...], normed)
    a, m, b = (steps[0, k].astype(F32) / 1000.0 for k in range(3))
    if t == 0:
        result[...] = latent[...] + (m - a) * velocity
    else:
        fine = latent[...] + (b - m) * velocity
        segment = lax.axis_index("seg")
        offset = jnp.where(segment == 0, fine, fine - b / a * rest[0][...])
        result[...] = offset / b


def prefix_sum(value, axis):
    count, mine = lax.axis_size(axis), lax.axis_index(axis)
    total = running = value
    base = 1
    while base < count:
        ways = 4 if count // base % 4 == 0 else 2
        place = mine // base % ways
        came = []
        for flip in (1, 3, 2)[: ways - 1]:
            pairs = []
            for s in range(count):
                partner = s ^ (flip * base)
                if ways == 2 and base > 1:
                    partner = s ^ (2 * base - base // 4)
                pairs.append((s, partner))
            came.append((flip, lax.ppermute(total, axis, pairs)))
        for flip, part in came:
            running = running + jnp.where((place ^ flip) < place, part, 0.0)
        for _, part in came:
            total = total + part
        base *= ways
    return running


VMEM = pl.BlockSpec(memory_space=pltpu.VMEM)
SMEM = pl.BlockSpec(memory_space=pltpu.SMEM)
ANY = pl.BlockSpec(memory_space=pl.ANY)


def per_device(
    latents, steps, text_hidden, text_len, embed_in, time_proj, qkv_image, kv_text, out_proj, embed_out
):
    model, _, width = qkv_image.shape
    slots = text_hidden.shape[0]
    channels = embed_in.shape[0]
    tokens = latents.shape[1]
    swap = [(0, 1), (1, 0)]
    half = time_proj.shape[0] // 2
    mixed = 2 * channels + AUX
    frequency = np.exp(-math.log(10000.0) * np.arange(half) / half).astype(np.float32)[None]
    latent = latents[0].T
    other = lax.ppermute(latent, "seq", swap)
    proj_other = lax.ppermute(out_proj, "seq", swap)
    embed_out_t = embed_out.T
    qkv_weights = jnp.transpose(qkv_image, (1, 0, 2))

    def call(kernel, name, outs, in_specs, scratch, limit, *args):
        return pl.pallas_call(
            kernel,
            out_shape=[pltpu.VMEM(dims, dtype) for dims, dtype in outs],
            in_specs=in_specs,
            out_specs=[VMEM] * len(outs),
            scratch_shapes=scratch,
            compiler_params=pltpu.CompilerParams(vmem_limit_bytes=limit << 20),
            name=name,
        )(*args)

    mixed_embed, mixed_in, key0, key1, val0, val1 = call(
        prepare_kernel,
        "prepare",
        [((mixed, model), BF16), ((mixed, 3 * width), BF16)] + [((slots, width), BF16)] * 4,
        [SMEM, SMEM, VMEM] + [ANY] * 5,
        [
            pltpu.VMEM(time_proj.shape, BF16),
            pltpu.VMEM(embed_in.shape, BF16),
            pltpu.VMEM((slots + AUX, model), BF16),
            pltpu.VMEM((3 * width // CHUNK, model, CHUNK), BF16),
            pltpu.VMEM(kv_text.shape, BF16),
            pltpu.VMEM((2, model, width), BF16),
            pltpu.VMEM((channels + AUX, model), BF16),
            pltpu.VMEM((2, slots, 128), F32),
            pltpu.SemaphoreType.DMA((3 + 6 * width // CHUNK,)),
        ],
        52,
        *(steps, text_len, frequency, time_proj, embed_in, text_hidden, qkv_weights, kv_text),
    )

    def evaluate(t, mine, other, text_key, text_val, *start):
        qkv, theirs = call(
            lambda *refs: theirs_kernel(t, *refs),
            "theirs",
            [((2 * tokens, 3 * width), BF16), ((tokens, width), BF16)],
            [SMEM] + [VMEM] * 6,
            [],
            16,
            *(text_len, mine, other, mixed_embed, mixed_in, text_key, text_val),
        )
        came = lax.ppermute(theirs, "seq", swap)
        (residual,) = call(
            lambda *refs: mine_kernel(t, *refs),
            "mine",
            [((tokens, model), F32)],
            [SMEM] + [VMEM] * 6,
            [pltpu.VMEM((tokens, width), BF16)],
            16,
            *(text_len, qkv, mine, mixed_embed, text_key, text_val, out_proj),
        )
        (result,) = call(
            lambda *refs: output_kernel(t, *refs),
            "output",
            [((channels, tokens), F32)],
            [SMEM] + [VMEM] * (5 + len(start)),
            [],
            16,
            *(steps, residual, came, mine, proj_other, embed_out_t, *start),
        )
        return result

    middle = evaluate(0, latent, other, key0, val0)
    offset = evaluate(1, middle, lax.ppermute(middle, "seq", swap), key1, val1, latent)
    result = steps[0, 2].astype(F32) / 1000.0 * prefix_sum(offset, "seg")
    return result.T[None]


def solution(mesh):
    return jax.shard_map(
        per_device,
        mesh=mesh,
        in_specs=(
            P("seg", "seq", None),
            P("seg", None),
            P(),
            P(),
            P(),
            P(),
            P(None, None, "seq"),
            P(None, None, "seq"),
            P("seq", None),
            P(),
        ),
        out_specs=P("seg", "seq", None),
        check_vma=False,
    )
```

```python
import math

import jax
import jax.numpy as jnp
import numpy as np
from jax import lax
from jax.experimental import pallas as pl
from jax.experimental.pallas import tpu as pltpu
from jax.sharding import PartitionSpec as P

HD = 64
CHUNK = 256
AUX = 16
epsilon = 1e-06
F32 = jnp.float32
BF16 = jnp.bfloat16


def dot(a, b):
    return jnp.dot(a, b, preferred_element_type=F32)


def dot_t(a, b):
    return lax.dot_general(a, b, (((1,), (1,)), ((), ())), preferred_element_type=F32)


def row_stats(x):
    mean = jnp.mean(x, -1, keepdims=True)
    centred = x - mean
    return mean, lax.rsqrt(jnp.mean(centred * centred, -1, keepdims=True) + epsilon)


def head_means():
    row = lax.broadcasted_iota(jnp.int32, (CHUNK, CHUNK), 0) // HD
    col = lax.broadcasted_iota(jnp.int32, (CHUNK, CHUNK), 1) // HD
    return jnp.where(row == col, 1.0 / HD, 0.0).astype(BF16)


def head_scale(y, means, scale):
    square = y * y
    high = square.astype(BF16)
    low = (square - high.astype(F32)).astype(BF16)
    mean = dot(high, means) + dot(low, means)
    return scale * lax.rsqrt(mean * (scale * scale) + epsilon)


def split(x):
    high = x.astype(BF16)
    return high, (x - high.astype(F32)).astype(BF16)


def time_rows(x, fifth=0.0):
    high, low = (part.astype(F32) for part in split(x))
    row = lax.broadcasted_iota(jnp.int32, (AUX, 1), 0)
    parts = (high[:1], low[:1], high[1:], low[1:], fifth)
    out = jnp.zeros((AUX, x.shape[1]), F32)
    for k, part in enumerate(parts):
        out = jnp.where(row == k, part, out)
    return out.astype(BF16)


def latent_rows(t, latent):
    z = latent.T.astype(BF16)
    col = lax.broadcasted_iota(jnp.int32, (z.shape[0], AUX), 1)
    pick = jnp.where(col // 2 == t, 1.0, 0.0).astype(BF16)
    return jnp.concatenate([z, z, pick], 1)


def prepare_kernel(
    steps, text_len, frequency, time_proj, embed_in, text, qkv, kv,
    mixed_embed, mixed_in, key0, key1, val0, val1,
    time_buf, embed_buf, text_rows, qkv_buf, kv_raw, kv_buf, embed_rows, stats, sems,
):
    parts = qkv.shape[2] // CHUNK
    slots, model = text.shape
    channels = embed_in.shape[0]
    small = [
        pltpu.make_async_copy(time_proj, time_buf, sems.at[0]),
        pltpu.make_async_copy(embed_in, embed_buf, sems.at[1]),
        pltpu.make_async_copy(text, text_rows.at[pl.ds(0, slots)], sems.at[2]),
    ]
    kv_rows = [(low, min(CHUNK, model - low)) for low in range(0, model, CHUNK)]
    kv_copies = []
    for i, (low, size) in enumerate(kv_rows):
        at = pl.ds(low, size)
        kv_copies.append(pltpu.make_async_copy(kv.at[at], kv_raw.at[at], sems.at[3 + i]))
    qkv_copies = []
    for i in range(3 * parts):
        qkv_copies.append(
            pltpu.make_async_copy(
                qkv.at[i // parts, :, pl.ds(i % parts * CHUNK, CHUNK)],
                qkv_buf.at[i],
                sems.at[3 + len(kv_rows) + i],
            )
        )
    for copy in small + kv_copies + qkv_copies:
        copy.start()
    means = head_means()
    row = lax.broadcasted_iota(jnp.int32, (AUX, 1), 0)
    t0, t1 = steps[0, 0].astype(F32), steps[0, 1].astype(F32)
    angle = jnp.where(row % 2 == 0, t0, t1) * frequency[...]
    emb = jnp.concatenate([jnp.cos(angle), jnp.sin(angle)], 1).astype(BF16)
    small[0].wait()
    time_vec = dot(emb, time_buf[...])
    high = time_vec.astype(BF16).astype(F32)
    aux = jnp.where(
        row < 2, high, jnp.where(row < 4, time_vec - high, jnp.where(row == 4, 1.0, 0.0))
    ).astype(BF16)
    time_mean = jnp.mean(time_vec[:2], -1, keepdims=True)
    time_centred = time_vec[:2] - time_mean
    of_times = jnp.mean(time_centred * time_centred, -1, keepdims=True)

    def store_mixed(ref, at, of_embed, of_time):
        high, low = split(of_embed)
        ref[:channels, at] = high
        ref[channels : 2 * channels, at] = low
        ref[2 * channels :, at] = time_rows(of_time)

    small[1].wait()
    embed = embed_buf[...]
    embed_rows[:channels] = embed
    embed_rows[channels:] = aux
    embed_mean = jnp.mean(embed.astype(F32), -1, keepdims=True)
    store_mixed(mixed_embed, slice(None), embed.astype(F32) - embed_mean, time_centred)

    text_rows[slots:] = aux
    small[2].wait()
    sums = dot_t(text_rows[:slots], time_rows(time_centred, 1.0))
    word_mean = sums[:, 4:5] * (1.0 / model)
    block = 48
    for i in range(slots // block):
        here = slice(i * block, (i + 1) * block)
        centred = text_rows[here].astype(F32) - word_mean[here]
        own = jnp.mean(centred * centred, -1, keepdims=True)
        for t in range(2):
            cross = (sums[here, 2 * t : 2 * t + 1] + sums[here, 2 * t + 1 : 2 * t + 2]) * (2.0 / model)
            scale = lax.rsqrt(own + cross + of_times[t : t + 1] + epsilon)
            stats[t, here] = jnp.broadcast_to(scale, (block, 128))

    live = lax.broadcasted_iota(jnp.int32, (slots, CHUNK), 0) < text_len[0]

    def text_project(i):
        return dot(text_rows[...], kv_buf[i // parts, :, i % parts * CHUNK : (i % parts + 1) * CHUNK])

    def text_store(i, out):
        at = slice(i % parts * CHUNK, (i % parts + 1) * CHUNK)
        ones = out[slots + 4 : slots + 5]
        base = out[:slots] - word_mean * ones
        for t in range(2):
            of_time = out[slots + t : slots + t + 1] + out[slots + 2 + t : slots + 3 + t]
            y = base + (of_time - time_mean[t : t + 1] * ones)
            scale = stats[t][:, :1]
            if i < parts:
                (key0, key1)[t][:, at] = (y * head_scale(y, means, scale)).astype(BF16)
            else:
                (val0, val1)[t][:, at] = jnp.where(live, y * scale, 0.0).astype(BF16)

    def image_chunk(i):
        at = slice(i * CHUNK, (i + 1) * CHUNK)
        out = dot(embed_rows[...], qkv_buf[i])
        ones = out[channels + 4 : channels + 5]
        of_time = out[channels : channels + 2] + out[channels + 2 : channels + 4]
        store_mixed(mixed_in, at, out[:channels] - embed_mean * ones, of_time - time_mean * ones)

    for copy in kv_copies:
        copy.wait()
    for low, size in kv_rows:
        kv_buf[:, low : low + size] = jnp.swapaxes(kv_raw[low : low + size], 0, 1)
    out = text_project(0)
    for i in range(2 * parts):
        later = text_project(i + 1) if i + 1 < 2 * parts else None
        text_store(i, out)
        out = later
    for copy in qkv_copies:
        copy.wait()
    for i in range(3 * parts):
        image_chunk(i)


def attend(qkv, rows, text_len, text_key, text_val, store):
    width = text_key.shape[1]
    slots = text_key.shape[0]
    tokens = rows.stop - rows.start
    pair_width = 2 * HD
    first = lax.broadcasted_iota(jnp.int32, (tokens, pair_width), 1) < HD
    live = (lax.broadcasted_iota(jnp.int32, (slots, pair_width), 0) < text_len[0]).astype(BF16)
    always = jnp.ones((qkv.shape[0], pair_width), BF16)
    pairs = width // pair_width

    def scores(pair):
        at = slice(pair * pair_width, (pair + 1) * pair_width)
        q = qkv[rows, at]
        both = jnp.concatenate([jnp.where(first, q, 0), jnp.where(first, 0, q)], 0)
        image_key = qkv[:, width + at.start : width + at.stop]
        return dot_t(both, image_key), dot_t(both, text_key[:, at])

    of_image, of_text = scores(0)
    for pair in range(pairs):
        later = scores(pair + 1) if pair + 1 < pairs else (None, None)
        at = slice(pair * pair_width, (pair + 1) * pair_width)
        image_val = qkv[:, 2 * width + at.start : 2 * width + at.stop]
        p_image = jnp.exp2(of_image).astype(BF16)
        p_text = jnp.exp2(of_text).astype(BF16)
        out = dot(p_image, jnp.concatenate([image_val, always], 1)) + dot(
            p_text, jnp.concatenate([text_val[:, at], live], 1)
        )
        out = out[:, :pair_width] / out[:, pair_width:]
        store(at, jnp.where(first, out[:tokens], out[tokens:]).astype(BF16))
        of_image, of_text = later


def theirs_kernel(
    t, text_len, mine, other, mixed_embed, mixed_in, text_key, text_val, qkv, out_other
):
    width = text_key.shape[1]
    tokens = mine.shape[1]
    rows = latent_rows(t, jnp.concatenate([mine[...], other[...]], 1))
    centred = dot(rows, mixed_embed[...])
    scale = lax.rsqrt(jnp.mean(centred * centred, -1, keepdims=True) + epsilon)
    means = head_means()
    chunks = 3 * width // CHUNK
    out = dot(rows, mixed_in[:, :CHUNK])
    for i in range(chunks):
        at = slice(i * CHUNK, (i + 1) * CHUNK)
        y = out
        if i + 1 < chunks:
            out = dot(rows, mixed_in[:, (i + 1) * CHUNK : (i + 2) * CHUNK])
        if i < 2 * width // CHUNK:
            of_head = head_scale(y, means, scale)
            if i < width // CHUNK:
                of_head = of_head * (math.log2(math.e) / math.sqrt(HD))
            y = y * of_head
        else:
            y = y * scale
        qkv[:, at] = y.astype(BF16)

    def store(at, value):
        out_other[:, at] = value

    attend(qkv, slice(tokens, 2 * tokens), text_len, text_key, text_val, store)


def mine_kernel(
    t, text_len, qkv, mine, mixed_embed, text_key, text_val, proj_mine, residual, attended
):
    tokens = mine.shape[1]

    def store(at, value):
        attended[:, at] = value

    attend(qkv, slice(0, tokens), text_len, text_key, text_val, store)
    rows = latent_rows(t, mine[...])
    residual[...] = dot(rows, mixed_embed[...]) + dot(attended[...], proj_mine[...])


def output_kernel(t, steps, residual, came, latent, proj_other, embed_out, *rest):
    result = rest[-1]
    whole = residual[...] + dot(came[...], proj_other[...])
    mean, scale = row_stats(whole)
    normed = ((whole - mean) * scale).astype(BF16)
    velocity = dot_t(embed_out[...], normed)
    a, m, b = (steps[0, k].astype(F32) / 1000.0 for k in range(3))
    if t == 0:
        result[...] = latent[...] + (m - a) * velocity
    else:
        fine = latent[...] + (b - m) * velocity
        segment = lax.axis_index("seg")
        offset = jnp.where(segment == 0, fine, fine - b / a * rest[0][...])
        result[...] = offset / b


def prefix_sum(value, axis):
    count, mine = lax.axis_size(axis), lax.axis_index(axis)
    total = running = value
    base = 1
    while base < count:
        ways = 4 if count // base % 4 == 0 else 2
        place = mine // base % ways
        came = []
        for flip in (1, 3, 2)[: ways - 1]:
            pairs = []
            for s in range(count):
                partner = s ^ (flip * base)
                if ways == 2 and base > 1:
                    partner = s ^ (2 * base - base // 4)
                pairs.append((s, partner))
            came.append((flip, lax.ppermute(total, axis, pairs)))
        for flip, part in came:
            running = running + jnp.where((place ^ flip) < place, part, 0.0)
        for _, part in came:
            total = total + part
        base *= ways
    return running


VMEM = pl.BlockSpec(memory_space=pltpu.VMEM)
SMEM = pl.BlockSpec(memory_space=pltpu.SMEM)
ANY = pl.BlockSpec(memory_space=pl.ANY)


def per_device(
    latents, steps, text_hidden, text_len, embed_in, time_proj, qkv_image, kv_text, out_proj, embed_out
):
    model, _, width = qkv_image.shape
    slots = text_hidden.shape[0]
    channels = embed_in.shape[0]
    tokens = latents.shape[1]
    swap = [(0, 1), (1, 0)]
    half = time_proj.shape[0] // 2
    mixed = 2 * channels + AUX
    frequency = np.exp(-math.log(10000.0) * np.arange(half) / half).astype(np.float32)[None]
    latent = latents[0].T
    other = lax.ppermute(latent, "seq", swap)
    proj_other = lax.ppermute(out_proj, "seq", swap)
    embed_out_t = embed_out.T
    qkv_weights = jnp.transpose(qkv_image, (1, 0, 2))

    def call(kernel, name, outs, in_specs, scratch, limit, *args):
        return pl.pallas_call(
            kernel,
            out_shape=[pltpu.VMEM(dims, dtype) for dims, dtype in outs],
            in_specs=in_specs,
            out_specs=[VMEM] * len(outs),
            scratch_shapes=scratch,
            compiler_params=pltpu.CompilerParams(vmem_limit_bytes=limit << 20),
            name=name,
        )(*args)

    mixed_embed, mixed_in, key0, key1, val0, val1 = call(
        prepare_kernel,
        "prepare",
        [((mixed, model), BF16), ((mixed, 3 * width), BF16)] + [((slots, width), BF16)] * 4,
        [SMEM, SMEM, VMEM] + [ANY] * 5,
        [
            pltpu.VMEM(time_proj.shape, BF16),
            pltpu.VMEM(embed_in.shape, BF16),
            pltpu.VMEM((slots + AUX, model), BF16),
            pltpu.VMEM((3 * width // CHUNK, model, CHUNK), BF16),
            pltpu.VMEM(kv_text.shape, BF16),
            pltpu.VMEM((2, model, width), BF16),
            pltpu.VMEM((channels + AUX, model), BF16),
            pltpu.VMEM((2, slots, 128), F32),
            pltpu.SemaphoreType.DMA((3 + 3 * width // CHUNK + -(-model // CHUNK),)),
        ],
        52,
        *(steps, text_len, frequency, time_proj, embed_in, text_hidden, qkv_weights, kv_text),
    )

    def evaluate(t, mine, other, text_key, text_val, *start):
        qkv, theirs = call(
            lambda *refs: theirs_kernel(t, *refs),
            "theirs",
            [((2 * tokens, 3 * width), BF16), ((tokens, width), BF16)],
            [SMEM] + [VMEM] * 6,
            [],
            16,
            *(text_len, mine, other, mixed_embed, mixed_in, text_key, text_val),
        )
        came = lax.ppermute(theirs, "seq", swap)
        (residual,) = call(
            lambda *refs: mine_kernel(t, *refs),
            "mine",
            [((tokens, model), F32)],
            [SMEM] + [VMEM] * 6,
            [pltpu.VMEM((tokens, width), BF16)],
            16,
            *(text_len, qkv, mine, mixed_embed, text_key, text_val, out_proj),
        )
        (result,) = call(
            lambda *refs: output_kernel(t, *refs),
            "output",
            [((channels, tokens), F32)],
            [SMEM] + [VMEM] * (5 + len(start)),
            [],
            16,
            *(steps, residual, came, mine, proj_other, embed_out_t, *start),
        )
        return result

    middle = evaluate(0, latent, other, key0, val0)
    offset = evaluate(1, middle, lax.ppermute(middle, "seq", swap), key1, val1, latent)
    result = steps[0, 2].astype(F32) / 1000.0 * prefix_sum(offset, "seg")
    return result.T[None]


def solution(mesh):
    return jax.shard_map(
        per_device,
        mesh=mesh,
        in_specs=(
            P("seg", "seq", None),
            P("seg", None),
            P(),
            P(),
            P(),
            P(),
            P(None, None, "seq"),
            P(None, None, "seq"),
            P("seq", None),
            P(),
        ),
        out_specs=P("seg", "seq", None),
        check_vma=False,
    )
```

```python
import math

import jax
import jax.numpy as jnp
import numpy as np
from jax import lax
from jax.experimental import pallas as pl
from jax.experimental.pallas import tpu as pltpu
from jax.sharding import PartitionSpec as P

HD = 64
CHUNK = 256
AUX = 16
epsilon = 1e-06
F32 = jnp.float32
BF16 = jnp.bfloat16


def dot(a, b):
    return jnp.dot(a, b, preferred_element_type=F32)


def dot_t(a, b):
    return lax.dot_general(a, b, (((1,), (1,)), ((), ())), preferred_element_type=F32)


def row_stats(x):
    mean = jnp.mean(x, -1, keepdims=True)
    centred = x - mean
    return mean, lax.rsqrt(jnp.mean(centred * centred, -1, keepdims=True) + epsilon)


def head_means():
    row = lax.broadcasted_iota(jnp.int32, (CHUNK, CHUNK), 0) // HD
    col = lax.broadcasted_iota(jnp.int32, (CHUNK, CHUNK), 1) // HD
    return jnp.where(row == col, 1.0 / HD, 0.0).astype(BF16)


def head_scale(y, means, scale):
    square = y * y
    high = square.astype(BF16)
    low = (square - high.astype(F32)).astype(BF16)
    mean = dot(high, means) + dot(low, means)
    return scale * lax.rsqrt(mean * (scale * scale) + epsilon)


def split(x):
    high = x.astype(BF16)
    return high, (x - high.astype(F32)).astype(BF16)


def time_rows(x, fifth=0.0):
    high, low = (part.astype(F32) for part in split(x))
    row = lax.broadcasted_iota(jnp.int32, (AUX, 1), 0)
    parts = (high[:1], low[:1], high[1:], low[1:], fifth)
    out = jnp.zeros((AUX, x.shape[1]), F32)
    for k, part in enumerate(parts):
        out = jnp.where(row == k, part, out)
    return out.astype(BF16)


def latent_rows(t, latent):
    z = latent.T.astype(BF16)
    col = lax.broadcasted_iota(jnp.int32, (z.shape[0], AUX), 1)
    pick = jnp.where(col // 2 == t, 1.0, 0.0).astype(BF16)
    return jnp.concatenate([z, z, pick], 1)


def prepare_kernel(
    steps, text_len, frequency, time_proj, embed_in, text, qkv, kv,
    mixed_embed, mixed_in, key0, key1, val0, val1,
    time_buf, embed_buf, text_rows, qkv_buf, kv_raw, kv_buf, embed_rows, stats, sems,
):
    parts = qkv.shape[2] // CHUNK
    slots, model = text.shape
    channels = embed_in.shape[0]
    small = [
        pltpu.make_async_copy(time_proj, time_buf, sems.at[0]),
        pltpu.make_async_copy(embed_in, embed_buf, sems.at[1]),
        pltpu.make_async_copy(text, text_rows.at[pl.ds(0, slots)], sems.at[2]),
    ]
    kv_rows = [(low, min(CHUNK, model - low)) for low in range(0, model, CHUNK)]
    kv_copies = []
    for i, (low, size) in enumerate(kv_rows):
        at = pl.ds(low, size)
        kv_copies.append(pltpu.make_async_copy(kv.at[at], kv_raw.at[at], sems.at[3 + i]))
    qkv_copies = []
    for i in range(3 * parts):
        qkv_copies.append(
            pltpu.make_async_copy(
                qkv.at[i // parts, :, pl.ds(i % parts * CHUNK, CHUNK)],
                qkv_buf.at[i],
                sems.at[3 + len(kv_rows) + i],
            )
        )
    for copy in small + kv_copies + qkv_copies:
        copy.start()
    means = head_means()
    row = lax.broadcasted_iota(jnp.int32, (AUX, 1), 0)
    t0, t1 = steps[0, 0].astype(F32), steps[0, 1].astype(F32)
    angle = jnp.where(row % 2 == 0, t0, t1) * frequency[...]
    emb = jnp.concatenate([jnp.cos(angle), jnp.sin(angle)], 1).astype(BF16)
    small[0].wait()
    time_vec = dot(emb, time_buf[...])
    high = time_vec.astype(BF16).astype(F32)
    aux = jnp.where(
        row < 2, high, jnp.where(row < 4, time_vec - high, jnp.where(row == 4, 1.0, 0.0))
    ).astype(BF16)
    time_mean = jnp.mean(time_vec[:2], -1, keepdims=True)
    time_centred = time_vec[:2] - time_mean
    of_times = jnp.mean(time_centred * time_centred, -1, keepdims=True)

    def store_mixed(ref, at, of_embed, of_time):
        high, low = split(of_embed)
        ref[:channels, at] = high
        ref[channels : 2 * channels, at] = low
        ref[2 * channels :, at] = time_rows(of_time)

    small[1].wait()
    embed = embed_buf[...]
    embed_rows[:channels] = embed
    embed_rows[channels:] = aux
    embed_mean = jnp.mean(embed.astype(F32), -1, keepdims=True)
    store_mixed(mixed_embed, slice(None), embed.astype(F32) - embed_mean, time_centred)

    text_rows[slots:] = aux
    small[2].wait()
    sums = dot_t(text_rows[:slots], time_rows(time_centred, 1.0))
    word_mean = sums[:, 4:5] * (1.0 / model)
    block = 48
    for i in range(slots // block):
        here = slice(i * block, (i + 1) * block)
        centred = text_rows[here].astype(F32) - word_mean[here]
        own = jnp.mean(centred * centred, -1, keepdims=True)
        for t in range(2):
            cross = (sums[here, 2 * t : 2 * t + 1] + sums[here, 2 * t + 1 : 2 * t + 2]) * (2.0 / model)
            scale = lax.rsqrt(own + cross + of_times[t : t + 1] + epsilon)
            stats[t, here] = jnp.broadcast_to(scale, (block, 128))

    live = lax.broadcasted_iota(jnp.int32, (slots, CHUNK), 0) < text_len[0]

    def text_project(i):
        return dot(text_rows[...], kv_buf[i // parts, :, i % parts * CHUNK : (i % parts + 1) * CHUNK])

    def text_store(i, out):
        at = slice(i % parts * CHUNK, (i % parts + 1) * CHUNK)
        ones = out[slots + 4 : slots + 5]
        base = out[:slots] - word_mean * ones
        for t in range(2):
            of_time = out[slots + t : slots + t + 1] + out[slots + 2 + t : slots + 3 + t]
            y = base + (of_time - time_mean[t : t + 1] * ones)
            scale = stats[t][:, :1]
            if i < parts:
                (key0, key1)[t][:, at] = (y * head_scale(y, means, scale)).astype(BF16)
            else:
                (val0, val1)[t][:, at] = jnp.where(live, y * scale, 0.0).astype(BF16)

    def image_chunk(i):
        at = slice(i * CHUNK, (i + 1) * CHUNK)
        out = dot(embed_rows[...], qkv_buf[i])
        ones = out[channels + 4 : channels + 5]
        of_time = out[channels : channels + 2] + out[channels + 2 : channels + 4]
        store_mixed(mixed_in, at, out[:channels] - embed_mean * ones, of_time - time_mean * ones)

    for copy in kv_copies:
        copy.wait()
    for low, size in kv_rows:
        kv_buf[:, low : low + size] = jnp.swapaxes(kv_raw[low : low + size], 0, 1)
    out = text_project(0)
    for i in range(2 * parts):
        later = text_project(i + 1) if i + 1 < 2 * parts else None
        text_store(i, out)
        out = later
    for copy in qkv_copies:
        copy.wait()
    for i in range(3 * parts):
        image_chunk(i)


def attend(qkv, rows, text_len, text_key, text_val, store):
    width = text_key.shape[1]
    slots = text_key.shape[0]
    tokens = rows.stop - rows.start
    pair_width = 2 * HD
    first = lax.broadcasted_iota(jnp.int32, (tokens, pair_width), 1) < HD
    live = (lax.broadcasted_iota(jnp.int32, (slots, pair_width), 0) < text_len[0]).astype(BF16)
    always = jnp.ones((qkv.shape[0], pair_width), BF16)
    pairs = width // pair_width

    def scores(pair):
        at = slice(pair * pair_width, (pair + 1) * pair_width)
        q = qkv[rows, at]
        both = jnp.concatenate([jnp.where(first, q, 0), jnp.where(first, 0, q)], 0)
        image_key = qkv[:, width + at.start : width + at.stop]
        return dot_t(both, image_key), dot_t(both, text_key[:, at])

    of_image, of_text = scores(0)
    for pair in range(pairs):
        later = scores(pair + 1) if pair + 1 < pairs else (None, None)
        at = slice(pair * pair_width, (pair + 1) * pair_width)
        image_val = qkv[:, 2 * width + at.start : 2 * width + at.stop]
        p_image = jnp.exp2(of_image).astype(BF16)
        p_text = jnp.exp2(of_text).astype(BF16)
        out = dot(p_image, jnp.concatenate([image_val, always], 1)) + dot(
            p_text, jnp.concatenate([text_val[:, at], live], 1)
        )
        out = out[:, :pair_width] / out[:, pair_width:]
        store(at, jnp.where(first, out[:tokens], out[tokens:]).astype(BF16))
        of_image, of_text = later


def theirs_kernel(
    t, text_len, mine, other, mixed_embed, mixed_in, text_key, text_val, qkv, out_other
):
    width = text_key.shape[1]
    tokens = mine.shape[1]
    rows = latent_rows(t, jnp.concatenate([mine[...], other[...]], 1))
    centred = dot(rows, mixed_embed[...])
    scale = lax.rsqrt(jnp.mean(centred * centred, -1, keepdims=True) + epsilon)
    means = head_means()
    chunks = 3 * width // CHUNK
    out = dot(rows, mixed_in[:, :CHUNK])
    for i in range(chunks):
        at = slice(i * CHUNK, (i + 1) * CHUNK)
        y = out
        if i + 1 < chunks:
            out = dot(rows, mixed_in[:, (i + 1) * CHUNK : (i + 2) * CHUNK])
        if i < 2 * width // CHUNK:
            of_head = head_scale(y, means, scale)
            if i < width // CHUNK:
                of_head = of_head * (math.log2(math.e) / math.sqrt(HD))
            y = y * of_head
        else:
            y = y * scale
        qkv[:, at] = y.astype(BF16)

    def store(at, value):
        out_other[:, at] = value

    attend(qkv, slice(tokens, 2 * tokens), text_len, text_key, text_val, store)


def mine_kernel(
    t, text_len, qkv, mine, mixed_embed, text_key, text_val, proj_mine, residual, attended
):
    tokens = mine.shape[1]

    def store(at, value):
        attended[:, at] = value

    attend(qkv, slice(0, tokens), text_len, text_key, text_val, store)
    rows = latent_rows(t, mine[...])
    residual[...] = dot(rows, mixed_embed[...]) + dot(attended[...], proj_mine[...])


def output_kernel(t, steps, residual, came, latent, proj_other, embed_out, *rest):
    result = rest[-1]
    whole = residual[...] + dot(came[...], proj_other[...])
    mean, scale = row_stats(whole)
    normed = ((whole - mean) * scale).astype(BF16)
    velocity = dot_t(embed_out[...], normed)
    a, m, b = (steps[0, k].astype(F32) / 1000.0 for k in range(3))
    if t == 0:
        result[...] = latent[...] + (m - a) * velocity
    else:
        fine = latent[...] + (b - m) * velocity
        segment = lax.axis_index("seg")
        offset = jnp.where(segment == 0, fine, fine - b / a * rest[0][...])
        result[...] = offset / b


def prefix_sum(value, axis):
    count, mine = lax.axis_size(axis), lax.axis_index(axis)
    total = running = value
    base = 1
    while base < count:
        ways = 4 if count // base % 4 == 0 else 2
        place = mine // base % ways
        came = []
        for flip in (2, 3, 1)[4 - ways :]:
            pairs = []
            for s in range(count):
                partner = s ^ (flip * base)
                if ways == 2 and base > 1:
                    partner = s ^ (2 * base - base // 4)
                pairs.append((s, partner))
            came.append((flip, lax.ppermute(total, axis, pairs)))
        for flip, part in came:
            running = running + jnp.where((place ^ flip) < place, part, 0.0)
        for _, part in came:
            total = total + part
        base *= ways
    return running


VMEM = pl.BlockSpec(memory_space=pltpu.VMEM)
SMEM = pl.BlockSpec(memory_space=pltpu.SMEM)
ANY = pl.BlockSpec(memory_space=pl.ANY)


def per_device(
    latents, steps, text_hidden, text_len, embed_in, time_proj, qkv_image, kv_text, out_proj, embed_out
):
    model, _, width = qkv_image.shape
    slots = text_hidden.shape[0]
    channels = embed_in.shape[0]
    tokens = latents.shape[1]
    swap = [(0, 1), (1, 0)]
    half = time_proj.shape[0] // 2
    mixed = 2 * channels + AUX
    frequency = np.exp(-math.log(10000.0) * np.arange(half) / half).astype(np.float32)[None]
    latent = latents[0].T
    other = lax.ppermute(latent, "seq", swap)
    proj_other = lax.ppermute(out_proj, "seq", swap)
    embed_out_t = embed_out.T
    qkv_weights = jnp.transpose(qkv_image, (1, 0, 2))

    def call(kernel, name, outs, in_specs, scratch, limit, *args):
        return pl.pallas_call(
            kernel,
            out_shape=[pltpu.VMEM(dims, dtype) for dims, dtype in outs],
            in_specs=in_specs,
            out_specs=[VMEM] * len(outs),
            scratch_shapes=scratch,
            compiler_params=pltpu.CompilerParams(vmem_limit_bytes=limit << 20),
            name=name,
        )(*args)

    mixed_embed, mixed_in, key0, key1, val0, val1 = call(
        prepare_kernel,
        "prepare",
        [((mixed, model), BF16), ((mixed, 3 * width), BF16)] + [((slots, width), BF16)] * 4,
        [SMEM, SMEM, VMEM] + [ANY] * 5,
        [
            pltpu.VMEM(time_proj.shape, BF16),
            pltpu.VMEM(embed_in.shape, BF16),
            pltpu.VMEM((slots + AUX, model), BF16),
            pltpu.VMEM((3 * width // CHUNK, model, CHUNK), BF16),
            pltpu.VMEM(kv_text.shape, BF16),
            pltpu.VMEM((2, model, width), BF16),
            pltpu.VMEM((channels + AUX, model), BF16),
            pltpu.VMEM((2, slots, 128), F32),
            pltpu.SemaphoreType.DMA((3 + 3 * width // CHUNK + -(-model // CHUNK),)),
        ],
        52,
        *(steps, text_len, frequency, time_proj, embed_in, text_hidden, qkv_weights, kv_text),
    )

    def evaluate(t, mine, other, text_key, text_val, *start):
        qkv, theirs = call(
            lambda *refs: theirs_kernel(t, *refs),
            "theirs",
            [((2 * tokens, 3 * width), BF16), ((tokens, width), BF16)],
            [SMEM] + [VMEM] * 6,
            [],
            16,
            *(text_len, mine, other, mixed_embed, mixed_in, text_key, text_val),
        )
        came = lax.ppermute(theirs, "seq", swap)
        (residual,) = call(
            lambda *refs: mine_kernel(t, *refs),
            "mine",
            [((tokens, model), F32)],
            [SMEM] + [VMEM] * 6,
            [pltpu.VMEM((tokens, width), BF16)],
            16,
            *(text_len, qkv, mine, mixed_embed, text_key, text_val, out_proj),
        )
        (result,) = call(
            lambda *refs: output_kernel(t, *refs),
            "output",
            [((channels, tokens), F32)],
            [SMEM] + [VMEM] * (5 + len(start)),
            [],
            16,
            *(steps, residual, came, mine, proj_other, embed_out_t, *start),
        )
        return result

    middle = evaluate(0, latent, other, key0, val0)
    offset = evaluate(1, middle, lax.ppermute(middle, "seq", swap), key1, val1, latent)
    result = steps[0, 2].astype(F32) / 1000.0 * prefix_sum(offset, "seg")
    return result.T[None]


def solution(mesh):
    return jax.shard_map(
        per_device,
        mesh=mesh,
        in_specs=(
            P("seg", "seq", None),
            P("seg", None),
            P(),
            P(),
            P(),
            P(),
            P(None, None, "seq"),
            P(None, None, "seq"),
            P("seq", None),
            P(),
        ),
        out_specs=P("seg", "seq", None),
        check_vma=False,
    )
```

```python
import math

import jax
import jax.numpy as jnp
import numpy as np
from jax import lax
from jax.experimental import pallas as pl
from jax.experimental.pallas import tpu as pltpu
from jax.sharding import PartitionSpec as P

HD = 64
CHUNK = 256
AUX = 16
epsilon = 1e-06
F32 = jnp.float32
BF16 = jnp.bfloat16


def dot(a, b):
    return jnp.dot(a, b, preferred_element_type=F32)


def dot_t(a, b):
    return lax.dot_general(a, b, (((1,), (1,)), ((), ())), preferred_element_type=F32)


def row_stats(x):
    mean = jnp.mean(x, -1, keepdims=True)
    centred = x - mean
    return mean, lax.rsqrt(jnp.mean(centred * centred, -1, keepdims=True) + epsilon)


def head_means():
    row = lax.broadcasted_iota(jnp.int32, (CHUNK, CHUNK), 0) // HD
    col = lax.broadcasted_iota(jnp.int32, (CHUNK, CHUNK), 1) // HD
    return jnp.where(row == col, 1.0 / HD, 0.0).astype(BF16)


def head_scale(y, means, scale):
    square = y * y
    high = square.astype(BF16)
    low = (square - high.astype(F32)).astype(BF16)
    mean = dot(high, means) + dot(low, means)
    return scale * lax.rsqrt(mean * (scale * scale) + epsilon)


def split(x):
    high = x.astype(BF16)
    return high, (x - high.astype(F32)).astype(BF16)


def time_rows(x, fifth=0.0):
    high, low = (part.astype(F32) for part in split(x))
    row = lax.broadcasted_iota(jnp.int32, (AUX, 1), 0)
    parts = (high[:1], low[:1], high[1:], low[1:], fifth)
    out = jnp.zeros((AUX, x.shape[1]), F32)
    for k, part in enumerate(parts):
        out = jnp.where(row == k, part, out)
    return out.astype(BF16)


def latent_rows(t, latent):
    z = latent.T.astype(BF16)
    col = lax.broadcasted_iota(jnp.int32, (z.shape[0], AUX), 1)
    pick = jnp.where(col // 2 == t, 1.0, 0.0).astype(BF16)
    return jnp.concatenate([z, z, pick], 1)


def prepare_kernel(
    steps, text_len, frequency, time_proj, embed_in, text, qkv, kv,
    mixed_embed, mixed_in, key0, key1, val0, val1,
    time_buf, embed_buf, text_rows, qkv_buf, kv_raw, kv_buf, embed_rows, stats, sems,
):
    parts = qkv.shape[2] // CHUNK
    slots, model = text.shape
    channels = embed_in.shape[0]
    small = [
        pltpu.make_async_copy(time_proj, time_buf, sems.at[0]),
        pltpu.make_async_copy(embed_in, embed_buf, sems.at[1]),
        pltpu.make_async_copy(text, text_rows.at[pl.ds(0, slots)], sems.at[2]),
    ]
    kv_rows = [(low, min(CHUNK, model - low)) for low in range(0, model, CHUNK)]
    kv_copies = []
    for i, (low, size) in enumerate(kv_rows):
        at = pl.ds(low, size)
        kv_copies.append(pltpu.make_async_copy(kv.at[at], kv_raw.at[at], sems.at[3 + i]))
    qkv_copies = []
    for i in range(3 * parts):
        qkv_copies.append(
            pltpu.make_async_copy(
                qkv.at[i // parts, :, pl.ds(i % parts * CHUNK, CHUNK)],
                qkv_buf.at[i],
                sems.at[3 + len(kv_rows) + i],
            )
        )
    for copy in small + kv_copies + qkv_copies:
        copy.start()
    means = head_means()
    row = lax.broadcasted_iota(jnp.int32, (AUX, 1), 0)
    t0, t1 = steps[0, 0].astype(F32), steps[0, 1].astype(F32)
    angle = jnp.where(row % 2 == 0, t0, t1) * frequency[...]
    emb = jnp.concatenate([jnp.cos(angle), jnp.sin(angle)], 1).astype(BF16)
    small[0].wait()
    time_vec = dot(emb, time_buf[...])
    high = time_vec.astype(BF16).astype(F32)
    aux = jnp.where(
        row < 2, high, jnp.where(row < 4, time_vec - high, jnp.where(row == 4, 1.0, 0.0))
    ).astype(BF16)
    time_mean = jnp.mean(time_vec[:2], -1, keepdims=True)
    time_centred = time_vec[:2] - time_mean
    of_times = jnp.mean(time_centred * time_centred, -1, keepdims=True)

    def store_mixed(ref, at, of_embed, of_time):
        high, low = split(of_embed)
        ref[:channels, at] = high
        ref[channels : 2 * channels, at] = low
        ref[2 * channels :, at] = time_rows(of_time)

    small[1].wait()
    embed = embed_buf[...]
    embed_rows[:channels] = embed
    embed_rows[channels:] = aux
    embed_mean = jnp.mean(embed.astype(F32), -1, keepdims=True)
    store_mixed(mixed_embed, slice(None), embed.astype(F32) - embed_mean, time_centred)

    text_rows[slots:] = aux
    small[2].wait()
    sums = dot_t(text_rows[:slots], time_rows(time_centred, 1.0))
    word_mean = sums[:, 4:5] * (1.0 / model)
    block = 48
    for i in range(slots // block):
        here = slice(i * block, (i + 1) * block)
        centred = text_rows[here].astype(F32) - word_mean[here]
        own = jnp.mean(centred * centred, -1, keepdims=True)
        for t in range(2):
            cross = (sums[here, 2 * t : 2 * t + 1] + sums[here, 2 * t + 1 : 2 * t + 2]) * (2.0 / model)
            scale = lax.rsqrt(own + cross + of_times[t : t + 1] + epsilon)
            stats[t, here] = jnp.broadcast_to(scale, (block, 128))

    live = lax.broadcasted_iota(jnp.int32, (slots, CHUNK), 0) < text_len[0]

    def text_project(i):
        return dot(text_rows[...], kv_buf[i // parts, :, i % parts * CHUNK : (i % parts + 1) * CHUNK])

    def text_store(i, out):
        at = slice(i % parts * CHUNK, (i % parts + 1) * CHUNK)
        ones = out[slots + 4 : slots + 5]
        base = out[:slots] - word_mean * ones
        for t in range(2):
            of_time = out[slots + t : slots + t + 1] + out[slots + 2 + t : slots + 3 + t]
            y = base + (of_time - time_mean[t : t + 1] * ones)
            scale = stats[t][:, :1]
            if i < parts:
                (key0, key1)[t][:, at] = (y * head_scale(y, means, scale)).astype(BF16)
            else:
                (val0, val1)[t][:, at] = jnp.where(live, y * scale, 0.0).astype(BF16)

    def image_chunk(i):
        at = slice(i * CHUNK, (i + 1) * CHUNK)
        out = dot(embed_rows[...], qkv_buf[i])
        ones = out[channels + 4 : channels + 5]
        of_time = out[channels : channels + 2] + out[channels + 2 : channels + 4]
        store_mixed(mixed_in, at, out[:channels] - embed_mean * ones, of_time - time_mean * ones)

    for copy in kv_copies:
        copy.wait()
    for low, size in kv_rows:
        kv_buf[:, low : low + size] = jnp.swapaxes(kv_raw[low : low + size], 0, 1)
    out = text_project(0)
    for i in range(2 * parts):
        later = text_project(i + 1) if i + 1 < 2 * parts else None
        text_store(i, out)
        out = later
    for copy in qkv_copies:
        copy.wait()
    for i in range(3 * parts):
        image_chunk(i)


def attend(qkv, rows, text_len, text_key, text_val, store):
    width = text_key.shape[1]
    slots = text_key.shape[0]
    tokens = rows.stop - rows.start
    pair_width = 2 * HD
    first = lax.broadcasted_iota(jnp.int32, (tokens, pair_width), 1) < HD
    live = (lax.broadcasted_iota(jnp.int32, (slots, pair_width), 0) < text_len[0]).astype(BF16)
    always = jnp.ones((qkv.shape[0], pair_width), BF16)
    pairs = width // pair_width

    def scores(pair):
        at = slice(pair * pair_width, (pair + 1) * pair_width)
        q = qkv[rows, at]
        both = jnp.concatenate([jnp.where(first, q, 0), jnp.where(first, 0, q)], 0)
        image_key = qkv[:, width + at.start : width + at.stop]
        return dot_t(both, image_key), dot_t(both, text_key[:, at])

    of_image, of_text = scores(0)
    for pair in range(pairs):
        later = scores(pair + 1) if pair + 1 < pairs else (None, None)
        at = slice(pair * pair_width, (pair + 1) * pair_width)
        image_val = qkv[:, 2 * width + at.start : 2 * width + at.stop]
        p_image = jnp.exp2(of_image).astype(BF16)
        p_text = jnp.exp2(of_text).astype(BF16)
        out = dot(p_image, jnp.concatenate([image_val, always], 1)) + dot(
            p_text, jnp.concatenate([text_val[:, at], live], 1)
        )
        out = out[:, :pair_width] / out[:, pair_width:]
        store(at, jnp.where(first, out[:tokens], out[tokens:]).astype(BF16))
        of_image, of_text = later


def theirs_kernel(
    t, text_len, mine, other, mixed_embed, mixed_in, text_key, text_val, qkv, out_other
):
    width = text_key.shape[1]
    tokens = mine.shape[1]
    rows = latent_rows(t, jnp.concatenate([mine[...], other[...]], 1))
    centred = dot(rows, mixed_embed[...])
    scale = lax.rsqrt(jnp.mean(centred * centred, -1, keepdims=True) + epsilon)
    means = head_means()
    chunks = 3 * width // CHUNK
    out = dot(rows, mixed_in[:, :CHUNK])
    for i in range(chunks):
        at = slice(i * CHUNK, (i + 1) * CHUNK)
        y = out
        if i + 1 < chunks:
            out = dot(rows, mixed_in[:, (i + 1) * CHUNK : (i + 2) * CHUNK])
        if i < 2 * width // CHUNK:
            of_head = head_scale(y, means, scale)
            if i < width // CHUNK:
                of_head = of_head * (math.log2(math.e) / math.sqrt(HD))
            y = y * of_head
        else:
            y = y * scale
        qkv[:, at] = y.astype(BF16)

    def store(at, value):
        out_other[:, at] = value

    attend(qkv, slice(tokens, 2 * tokens), text_len, text_key, text_val, store)


def mine_kernel(
    t, text_len, qkv, mine, mixed_embed, text_key, text_val, proj_mine, residual, attended
):
    tokens = mine.shape[1]

    def store(at, value):
        attended[:, at] = value

    attend(qkv, slice(0, tokens), text_len, text_key, text_val, store)
    rows = latent_rows(t, mine[...])
    residual[...] = dot(rows, mixed_embed[...]) + dot(attended[...], proj_mine[...])


def output_kernel(t, steps, residual, came, latent, proj_other, embed_out, *rest):
    result = rest[-1]
    model = residual.shape[1]
    cuts = [slice(low, min(low + 2 * CHUNK, model)) for low in range(0, model, 2 * CHUNK)]
    parts, total = [], 0.0
    out = dot(came[...], proj_other[:, cuts[0]])
    for k, cut in enumerate(cuts):
        later = dot(came[...], proj_other[:, cuts[k + 1]]) if k + 1 < len(cuts) else None
        parts.append(residual[:, cut] + out)
        total = total + jnp.sum(parts[-1], -1, keepdims=True)
        out = later
    mean = total / model
    spread = sum(jnp.sum((part - mean) * (part - mean), -1, keepdims=True) for part in parts)
    scale = lax.rsqrt(spread / model + epsilon)
    velocity = 0.0
    for cut, part in zip(cuts, parts):
        velocity = velocity + dot_t(embed_out[:, cut], ((part - mean) * scale).astype(BF16))
    a, m, b = (steps[0, k].astype(F32) / 1000.0 for k in range(3))
    if t == 0:
        result[...] = latent[...] + (m - a) * velocity
    else:
        fine = latent[...] + (b - m) * velocity
        segment = lax.axis_index("seg")
        offset = jnp.where(segment == 0, fine, fine - b / a * rest[0][...])
        result[...] = offset / b


def prefix_sum(value, axis):
    count, mine = lax.axis_size(axis), lax.axis_index(axis)
    total = running = value
    base = 1
    while base < count:
        ways = 4 if count // base % 4 == 0 else 2
        place = mine // base % ways
        came = []
        for flip in (2, 3, 1)[4 - ways :]:
            pairs = []
            for s in range(count):
                partner = s ^ (flip * base)
                if ways == 2 and base > 1:
                    partner = s ^ (2 * base - base // 4)
                pairs.append((s, partner))
            came.append((flip, lax.ppermute(total, axis, pairs)))
        for flip, part in came:
            running = running + jnp.where((place ^ flip) < place, part, 0.0)
        for _, part in came:
            total = total + part
        base *= ways
    return running


VMEM = pl.BlockSpec(memory_space=pltpu.VMEM)
SMEM = pl.BlockSpec(memory_space=pltpu.SMEM)
ANY = pl.BlockSpec(memory_space=pl.ANY)


def per_device(
    latents, steps, text_hidden, text_len, embed_in, time_proj, qkv_image, kv_text, out_proj, embed_out
):
    model, _, width = qkv_image.shape
    slots = text_hidden.shape[0]
    channels = embed_in.shape[0]
    tokens = latents.shape[1]
    swap = [(0, 1), (1, 0)]
    half = time_proj.shape[0] // 2
    mixed = 2 * channels + AUX
    frequency = np.exp(-math.log(10000.0) * np.arange(half) / half).astype(np.float32)[None]
    latent = latents[0].T
    other = lax.ppermute(latent, "seq", swap)
    proj_other = lax.ppermute(out_proj, "seq", swap)
    embed_out_t = embed_out.T
    qkv_weights = jnp.transpose(qkv_image, (1, 0, 2))

    def call(kernel, name, outs, in_specs, scratch, limit, *args):
        return pl.pallas_call(
            kernel,
            out_shape=[pltpu.VMEM(dims, dtype) for dims, dtype in outs],
            in_specs=in_specs,
            out_specs=[VMEM] * len(outs),
            scratch_shapes=scratch,
            compiler_params=pltpu.CompilerParams(vmem_limit_bytes=limit << 20),
            name=name,
        )(*args)

    mixed_embed, mixed_in, key0, key1, val0, val1 = call(
        prepare_kernel,
        "prepare",
        [((mixed, model), BF16), ((mixed, 3 * width), BF16)] + [((slots, width), BF16)] * 4,
        [SMEM, SMEM, VMEM] + [ANY] * 5,
        [
            pltpu.VMEM(time_proj.shape, BF16),
            pltpu.VMEM(embed_in.shape, BF16),
            pltpu.VMEM((slots + AUX, model), BF16),
            pltpu.VMEM((3 * width // CHUNK, model, CHUNK), BF16),
            pltpu.VMEM(kv_text.shape, BF16),
            pltpu.VMEM((2, model, width), BF16),
            pltpu.VMEM((channels + AUX, model), BF16),
            pltpu.VMEM((2, slots, 128), F32),
            pltpu.SemaphoreType.DMA((3 + 3 * width // CHUNK + -(-model // CHUNK),)),
        ],
        52,
        *(steps, text_len, frequency, time_proj, embed_in, text_hidden, qkv_weights, kv_text),
    )

    def evaluate(t, mine, other, text_key, text_val, *start):
        qkv, theirs = call(
            lambda *refs: theirs_kernel(t, *refs),
            "theirs",
            [((2 * tokens, 3 * width), BF16), ((tokens, width), BF16)],
            [SMEM] + [VMEM] * 6,
            [],
            16,
            *(text_len, mine, other, mixed_embed, mixed_in, text_key, text_val),
        )
        came = lax.ppermute(theirs, "seq", swap)
        (residual,) = call(
            lambda *refs: mine_kernel(t, *refs),
            "mine",
            [((tokens, model), F32)],
            [SMEM] + [VMEM] * 6,
            [pltpu.VMEM((tokens, width), BF16)],
            16,
            *(text_len, qkv, mine, mixed_embed, text_key, text_val, out_proj),
        )
        (result,) = call(
            lambda *refs: output_kernel(t, *refs),
            "output",
            [((channels, tokens), F32)],
            [SMEM] + [VMEM] * (5 + len(start)),
            [],
            16,
            *(steps, residual, came, mine, proj_other, embed_out_t, *start),
        )
        return result

    middle = evaluate(0, latent, other, key0, val0)
    offset = evaluate(1, middle, lax.ppermute(middle, "seq", swap), key1, val1, latent)
    result = steps[0, 2].astype(F32) / 1000.0 * prefix_sum(offset, "seg")
    return result.T[None]


def solution(mesh):
    return jax.shard_map(
        per_device,
        mesh=mesh,
        in_specs=(
            P("seg", "seq", None),
            P("seg", None),
            P(),
            P(),
            P(),
            P(),
            P(None, None, "seq"),
            P(None, None, "seq"),
            P("seq", None),
            P(),
        ),
        out_specs=P("seg", "seq", None),
        check_vma=False,
    )
```
